128 devices in a mesh: rep: 16 (over y_lo, z, core), shard: 8 (over x, y_hi).
Axes of the slice: x: 4, y: 4 (y_hi: 2, y_lo: 2; y = y_hi * 2 + y_lo), z: 4, core: 2. Of those that a mesh axis runs over, the one named last changes fastest.
Arguments:
- grads: bfloat16 [16, 8, 256, 22016], P('rep', 'shard'), may hold values from -6 to 6
- momentum: float32 [16, 256, 22016], P('rep', None, 'shard'), may hold values from -12 to 12
Outputs:
- new_momentum: float32 [16, 256, 22016], P('rep', None, 'shard')
- update: float32 [256, 22016], P(None, 'shard')
The draws below stay inside these ranges and needn't reach their ends.
All inputs are finite; a program needn't handle non-finite values.
Results may differ from the reference program's by a relative error of at most 0.0003.
Values sent between devices are 32-bit elements; how exact they have to be, the bound alone decides.
No kernel may reach another device: no remote copies, remote signals or barrier semaphores. Data moves between devices by JAX's collectives and lax.ppermute only.
A program may use at most 192 MiB of HBM per device.

```python
import jax
import jax.numpy as jnp
from jax import lax

FF = 22016
ROWS = 256
N_REP = 16
N_SHARD = 8


def spiked(result, rng, source, target, parts, factor):
    def block_of(dim):
        return (jnp.arange(result.shape[dim]) // (result.shape[dim] // parts)).reshape((-1,) + (1,) * (result.ndim - 1 - dim))

    near = jax.random.permutation(rng, parts)[block_of(target)]
    other_side = (block_of(target) + parts // 2) % parts
    return jnp.where((block_of(source) == near) | (block_of(source) == other_side), factor * result, result)


def levels(rng, dims, split, low, high):
    def one(dim, blocks):
        draws = jax.random.uniform(jax.random.fold_in(jax.random.fold_in(rng, 6), dim), (blocks,), jnp.float32, low / len(split), high / len(split))
        return jnp.repeat(jnp.exp(draws), dims[dim] // blocks).reshape((-1,) + (1,) * (len(dims) - dim - 1))

    factor_of = one(*split[0])
    for cut in split[1:]:
        factor_of = factor_of * one(*cut)
    return factor_of


def centred(rng, dims, deviation, most, shards=(), kind=jnp.bfloat16):
    gain = levels(rng, dims, shards, -0.22, 0.18) if shards else 1.0
    drawn = jax.random.normal(rng, dims, jnp.float32) * deviation * gain
    return jnp.minimum(jnp.maximum(drawn, -most), most).astype(kind)


def heavy_noise(key, extent, spread, reach, shards, heavy, kind=jnp.bfloat16):
    result = spread * jax.random.normal(key, extent, jnp.float32)
    if shards:
        result = result * levels(key, extent, shards, -0.22, 0.18)
    return jnp.clip(spiked(result, jax.random.fold_in(key, 3), *heavy), -reach, reach).astype(kind)


def setup_inputs(seed: int = 0) -> dict:
    streams_of = jax.random.split(jax.random.key(seed), 3)
    grads = heavy_noise(streams_of[0], (N_REP, N_SHARD, ROWS, FF), 1.0, 6.0, ((0, 16), (1, 8)), (1, 3, 8, 2.0))
    momentum = centred(streams_of[1], (N_REP, ROWS, FF), 2.0, 12.0, ((0, 16), (2, 8)), jnp.float32)
    return dict(grads=grads, momentum=momentum)


BETA = 0.9
SHARP = 4.0

def cosine_table():
    freqs = jnp.arange(16, dtype=jnp.float32)[:, None]
    points = jnp.arange(64, dtype=jnp.float32)[None, :]
    norming = jnp.where(freqs == 0.0, jnp.sqrt(jnp.float32(1.0 / 64.0)), jnp.sqrt(jnp.float32(2.0 / 64.0)))
    return norming * jnp.cos(jnp.pi * (2.0 * points + 1.0) * freqs / 128.0)

def transform(values, basis):
    row_blocks = values.shape[0] // 64
    blocks = values.reshape(row_blocks, 64, -1)
    rowwise = jnp.einsum('kn,anf->akf', basis, blocks, precision=lax.Precision.HIGHEST)
    rowwise = rowwise.reshape(row_blocks, 16, -1, 64)
    return jnp.einsum('akbm,lm->akbl', rowwise, basis, precision=lax.Precision.HIGHEST)

def restore(coeffs, basis):
    row_blocks = coeffs.shape[0]
    rowwise = jnp.einsum('akbl,lm->akbm', coeffs, basis, precision=lax.Precision.HIGHEST)
    rowwise = rowwise.reshape(row_blocks, 16, -1)
    output = jnp.einsum('kn,akf->anf', basis, rowwise, precision=lax.Precision.HIGHEST)
    return output.reshape(row_blocks * 64, -1)

def reference(grads, momentum):
    basis = cosine_table()

    def one_replica(inputs):
        partials, previous = inputs
        gradient = lax.optimization_barrier(jnp.sum(partials.astype(jnp.float32), axis=0))
        merged = BETA * previous + gradient
        coeffs = transform(merged, basis)
        return (merged - restore(coeffs, basis), coeffs)
    new_momentum, coeffs = lax.map(one_replica, (grads, momentum))
    average = lax.optimization_barrier(jnp.sum(coeffs, axis=0)) / N_REP
    update = jnp.tanh(SHARP * restore(average, basis))
    return (new_momentum, update)
```

```python
import functools

import jax
import jax.numpy as jnp
import numpy as np
from jax import lax
from jax.experimental import pallas as pl
from jax.experimental.pallas import tpu as pltpu
from jax.sharding import PartitionSpec as P

BETA = 0.9
SHARP = 4.0
ROWS = 256
LANES = 128
SUPER = 43
MID = 21
OWN = 22
NB = 9
NBP = 5
STEP_ROWS = 64

F32 = jnp.float32


def x_ring(step):
    return [(s, ((s // 2 + step) % 4) * 2 + s % 2) for s in range(8)]


Y_FLIP = [(s, s ^ 1) for s in range(8)]
CORE_FLIP = [(r, r ^ 1) for r in range(16)]
YLO_FLIP = [(r, r ^ 8) for r in range(16)]


def z_ring(step):
    return [(r, (r // 8) * 8 + ((r // 2 % 4 + step) % 4) * 2 + r % 2) for r in range(16)]


def up(value):
    return lax.ppermute(value, "shard", x_ring(1))


def down(value):
    return lax.ppermute(value, "shard", x_ring(-1))


def across(value):
    return lax.ppermute(value, "shard", Y_FLIP)


def grads_spec(slot, tiles):
    def where(row, starts):
        return row * STEP_ROWS, pl.multiple_of(starts[slot] * LANES, LANES)

    return pl.BlockSpec((pl.Element(STEP_ROWS), pl.Element(tiles * LANES)), where)


def rows_spec(tiles):
    return pl.BlockSpec((STEP_ROWS, tiles * LANES), lambda row, starts: (row, 0))


def rows_call(kernel, starts, ins, in_specs, out_tiles, bytes_moved):
    outs = [jax.ShapeDtypeStruct((ROWS, t * LANES), F32) for t in out_tiles]
    return pl.pallas_call(
        kernel,
        grid_spec=pltpu.PrefetchScalarGridSpec(
            num_scalar_prefetch=1,
            grid=(ROWS // STEP_ROWS,),
            in_specs=in_specs,
            out_specs=[rows_spec(t) for t in out_tiles],
        ),
        out_shape=outs,
        cost_estimate=pl.CostEstimate(
            flops=bytes_moved // 4, bytes_accessed=bytes_moved, transcendentals=0
        ),
    )(jnp.stack(starts).astype(jnp.int32), *ins)


def widen_kernel(counts, starts, *refs):
    n = sum(len(c) for c in counts)
    ins, outs = refs[:n], refs[n:]
    at = 0
    for out, group in zip(outs, counts):
        col = 0
        for tiles in group:
            out[:, col : col + tiles * LANES] = ins[at][...].astype(F32)
            col += tiles * LANES
            at += 1


def widen(grads, groups):
    counts = [[t for _, t in g] for g in groups]
    flat = [piece for g in groups for piece in g]
    total = sum(t for _, t in flat)
    return rows_call(
        functools.partial(widen_kernel, counts),
        [s for s, _ in flat],
        [grads] * len(flat),
        [grads_spec(k, t) for k, (_, t) in enumerate(flat)],
        [sum(c) for c in counts],
        total * LANES * ROWS * 6,
    )


def add_kernel(tiles, offsets, starts, g, *refs):
    out = refs[-1]
    total = g[...].astype(F32)
    for ref, off in zip(refs[:-1], offsets):
        total = total + ref[:, off * LANES : (off + tiles) * LANES]
    out[...] = total


def add(grads, start, tiles, parts):
    return rows_call(
        functools.partial(add_kernel, tiles, [o for _, o in parts]),
        [start],
        [grads] + [a for a, _ in parts],
        [grads_spec(0, tiles)] + [rows_spec(a.shape[1] // LANES) for a, _ in parts],
        [tiles],
        tiles * LANES * ROWS * (6 + 4 * len(parts)),
    )[0]


def cross_first_kernel(starts, g, plus, minus, out):
    @pl.when(starts[1] == 0)
    def _():
        out[...] = minus[...] + g[...].astype(F32)

    @pl.when(starts[1] == 1)
    def _():
        w = 6 * LANES
        out[:, :w] = plus[...] + g[:, :w].astype(F32)
        out[:, w:] = minus[:, :LANES] + g[:, w:].astype(F32)


def cross_second_kernel(starts, g, plus, minus, out):
    @pl.when(starts[1] == 0)
    def _():
        out[...] = minus[...] + g[...].astype(F32)

    @pl.when(starts[1] == 1)
    def _():
        out[...] = plus[...] + g[...].astype(F32)


def cross_call(kernel, grads, start, yh, tiles, plus, minus):
    return rows_call(
        kernel,
        [start, yh],
        [grads, plus, minus],
        [
            grads_spec(0, tiles),
            rows_spec(plus.shape[1] // LANES),
            rows_spec(minus.shape[1] // LANES),
        ],
        [tiles],
        tiles * LANES * ROWS * 14,
    )[0]


def half_roll(tile):
    return pltpu.roll(tile, 64, axis=1)


def base_kernel(starts, g, momentum, out):
    low = lax.broadcasted_iota(jnp.int32, (STEP_ROWS, LANES), 1) < 64

    @pl.when(starts[1] == 0)
    def _():
        for t in range(OWN):
            at = slice(t * LANES, (t + 1) * LANES)
            if t < OWN - 1:
                m = momentum[:, at]
            else:
                m = jnp.concatenate(
                    [momentum[:, t * LANES : t * LANES + 64], jnp.zeros((STEP_ROWS, 64), F32)], 1
                )
            total = BETA * m + g[:, at].astype(F32)
            if t == OWN - 1:
                total = jnp.where(low, total, 0.0)
            out[:, at] = total

    @pl.when(starts[1] == 1)
    def _():
        before = jnp.zeros((STEP_ROWS, LANES), F32)
        for t in range(OWN):
            at = slice(t * LANES, (t + 1) * LANES)
            if t < OWN - 1:
                m = half_roll(momentum[:, at])
            else:
                m = jnp.concatenate(
                    [jnp.zeros((STEP_ROWS, 64), F32), momentum[:, t * LANES : t * LANES + 64]], 1
                )
            total = BETA * jnp.where(low, before, m) + g[:, at].astype(F32)
            if t == 0:
                total = jnp.where(low, 0.0, total)
            out[:, at] = total
            before = m


def base_call(grads, momentum, start, yh):
    return rows_call(
        base_kernel,
        [start, yh],
        [grads, momentum],
        [
            grads_spec(0, OWN),
            pl.BlockSpec((STEP_ROWS, momentum.shape[1]), lambda row, starts: (row, 0)),
        ],
        [OWN],
        OWN * LANES * ROWS * 10,
    )[0]


def whole(*shape):
    return pl.BlockSpec(shape, lambda *_: (0,) * len(shape))


def dot(a, b):
    return lax.dot_general(
        a, b, (((1,), (0,)), ((), ())), precision=lax.Precision.HIGHEST, preferred_element_type=F32
    )


def mix_kernel(starts, base, pa, ma, ca, pb, mb, cb, bp, bm, rowmat, colmat, merged, coeffs):
    def put(tile, tiles, *sources):
        at = slice(tile * LANES, (tile + tiles) * LANES)
        total = base[:, at]
        for ref, off in sources:
            total = total + ref[:, off * LANES : (off + tiles) * LANES]
        merged[:, at] = total

    @pl.when(starts[0] == 0)
    def _():
        put(0, NBP, (bp, 0))
        put(NBP, NB - NBP, (bm, 0))
        put(9, 6, (pb, 0), (cb, 0))
        put(15, 6, (pa, 0), (ca, 0))
        put(21, 1, (ma, 0), (ca, 6))
        t = merged[:, 21 * LANES :]
        low = lax.broadcasted_iota(jnp.int32, t.shape, 1) < 64
        merged[:, 21 * LANES :] = jnp.where(low, t, 0.0)

    @pl.when(starts[0] == 1)
    def _():
        put(0, 7, (ma, 0), (ca, 0))
        put(7, 6, (mb, 0), (cb, 0))
        put(13, NBP, (bp, 0))
        put(13 + NBP, NB - NBP, (bm, 0))
        t = merged[:, :LANES]
        low = lax.broadcasted_iota(jnp.int32, t.shape, 1) < 64
        merged[:, :LANES] = jnp.where(low, 0.0, t)

    for t in range(0, OWN, 2):
        rowwise = dot(rowmat[...], merged[:, t * LANES : (t + 2) * LANES])
        coeffs[:, t * 32 : (t + 2) * 32] = dot(rowwise, colmat[...])


def expand(coeffs, rowmat_t, colmat_t):
    return dot(rowmat_t, dot(coeffs, colmat_t))


def pair_out(index, yh_is_one, tiles_of, out):
    width = out.shape[1]
    if not yh_is_one:
        for t in range(OWN):
            v = tiles_of(t)
            if t < OWN - 1:
                out[:, t * LANES : (t + 1) * LANES] = v
            else:
                out[:, t * LANES : width] = v[:, : width - t * LANES]
        return
    low = lax.broadcasted_iota(jnp.int32, (ROWS, LANES), 1) < 64
    ahead = half_roll(tiles_of(0))
    for t in range(OWN):
        if t < OWN - 1:
            following = half_roll(tiles_of(t + 1))
            out[:, t * LANES : (t + 1) * LANES] = jnp.where(low, ahead, following)
            ahead = following
        else:
            out[:, t * LANES : width] = ahead[:, : width - t * LANES]


def finish_kernel(starts, merged, coeffs, rowmat_t, colmat_t, out, full):
    for t in range(0, OWN, 2):
        at = slice(t * LANES, (t + 2) * LANES)
        full[:, at] = merged[:, at] - expand(
            coeffs[:, t * 32 : (t + 2) * 32], rowmat_t[...], colmat_t[...]
        )
    for yh in range(2):

        @pl.when(starts[0] == yh)
        def _():
            pair_out(None, yh == 1, lambda t: full[:, t * LANES : (t + 1) * LANES], out)


def update_kernel(starts, total, rowmat_t, colmat_t, out, full):
    for t in range(0, OWN, 2):
        at = slice(t * LANES, (t + 2) * LANES)
        decoded = expand(total[:, t * 32 : (t + 2) * 32], rowmat_t[...], colmat_t[...])
        full[:, at] = jnp.tanh(SHARP * decoded)
    for yh in range(2):

        @pl.when(starts[0] == yh)
        def _():
            pair_out(None, yh == 1, lambda t: full[:, t * LANES : (t + 1) * LANES], out)


def whole_call(kernel, starts, ins, outs, scratch, flops, moved):
    return pl.pallas_call(
        kernel,
        grid_spec=pltpu.PrefetchScalarGridSpec(
            num_scalar_prefetch=1,
            grid=(1,),
            in_specs=[whole(*a.shape) for a in ins],
            out_specs=[whole(*o) for o in outs],
            scratch_shapes=scratch,
        ),
        out_shape=[jax.ShapeDtypeStruct(o, F32) for o in outs],
        compiler_params=pltpu.CompilerParams(vmem_limit_bytes=48 << 20),
        cost_estimate=pl.CostEstimate(flops=flops, bytes_accessed=moved, transcendentals=0),
    )(jnp.stack(starts).astype(jnp.int32), *ins)


def cosine_table():
    freqs = np.arange(16, dtype=np.float64)[:, None]
    points = np.arange(64, dtype=np.float64)[None, :]
    norming = np.where(freqs == 0.0, np.sqrt(1.0 / 64.0), np.sqrt(2.0 / 64.0))
    return norming * np.cos(np.pi * (2.0 * points + 1.0) * freqs / 128.0)


def after(value, *others):
    return lax.optimization_barrier((value, *others))[0]


def local(grads, momentum):
    grads = grads[0, 0]
    momentum = momentum[0]
    shard = lax.axis_index("shard")
    x, yh = shard // 2, shard % 2
    other = 1 - yh

    def tile(dx, t):
        return ((x + dx) % 4) * SUPER + t

    b_own, b_other = 34 * yh, 34 * other

    def b_piece(k):
        return [(tile(-1 - k, b_other), NBP), (tile(1 + k, b_other + NBP), NB - NBP)]

    y0, pa, ma = widen(
        grads, [b_piece(0), [(tile(-1, 15), 6)], [(tile(1, 21), 7)]]
    )
    y0, pa, ma = across(y0), up(pa), down(ma)
    pb, mb, y1 = widen(grads, [[(tile(-1, 9), 6)], [(tile(1, 28), 6)], b_piece(1)])
    pb, mb, y1 = up(pb), down(mb), across(y1)
    y2, y3 = widen(grads, [b_piece(2), b_piece(3)])
    y2, y3 = across(y2), across(y3)
    ys = [y0, y1, y2, y3]

    base = base_call(grads, momentum, tile(0, MID * yh), yh)

    bp = bm = None
    for k in range(2):
        pa = up(add(grads, tile(-2 - k, 15), 6, [(pa, 0)]))
        ma = down(add(grads, tile(2 + k, 21), 7, [(ma, 0)]))
        pb = up(add(grads, tile(-2 - k, 9), 6, [(pb, 0)]))
        mb = down(add(grads, tile(2 + k, 28), 6, [(mb, 0)]))
    for k in range(3):
        bp = up(add(grads, tile(-1 - k, b_own), NBP, [(ys[k], 0)] + ([(bp, 0)] if k else [])))
        bm = down(
            add(grads, tile(1 + k, b_own + NBP), NB - NBP, [(ys[k], NBP)] + ([(bm, 0)] if k else []))
        )
    ca = across(cross_call(cross_first_kernel, grads, tile(0, 15 + 6 * other), yh, 7, pa, ma))
    cb = across(cross_call(cross_second_kernel, grads, tile(0, 9 + 19 * other), yh, 6, pb, mb))
    bp = add_plain(bp, ys[3], 0, NBP)
    bm = add_plain(bm, ys[3], NBP, NB - NBP)

    table = cosine_table()
    rowmat = jnp.asarray(np.kron(np.eye(4), table), F32)
    colmat = jnp.asarray(np.kron(np.eye(4), table.T), F32)
    rowmat_t = jnp.asarray(np.kron(np.eye(4), table.T), F32)
    colmat_t = jnp.asarray(np.kron(np.eye(4), table), F32)

    width = OWN * LANES
    merged, coeffs = whole_call(
        mix_kernel,
        [yh],
        [base, pa, ma, ca, pb, mb, cb, bp, bm, rowmat, colmat],
        [(ROWS, width), (64, width // 4)],
        [],
        2 * 64 * 256 * width * 6,
        ROWS * width * 16,
    )
    total = coeffs + lax.ppermute(coeffs, "rep", CORE_FLIP)
    total = (
        total
        + lax.ppermute(total, "rep", z_ring(1))
        + lax.ppermute(total, "rep", z_ring(-1))
        + lax.ppermute(total, "rep", z_ring(2))
    )
    total = total + lax.ppermute(total, "rep", YLO_FLIP)
    own = momentum.shape
    new_rows = whole_call(
        finish_kernel,
        [yh],
        [merged, coeffs, rowmat_t, colmat_t],
        [own],
        [pltpu.VMEM((ROWS, width), F32)],
        2 * 64 * 256 * width * 6,
        ROWS * width * 8,
    )[0]
    update = whole_call(
        update_kernel,
        [yh],
        [total / 16.0, rowmat_t, colmat_t],
        [own],
        [pltpu.VMEM((ROWS, width), F32)],
        2 * 64 * 256 * width * 6,
        ROWS * width * 4,
    )[0]
    return new_rows[None], update


def add_plain(value, piece, offset, tiles):
    return value + piece[:, offset * LANES : (offset + tiles) * LANES]


def solution(mesh):
    placed = (P("rep", "shard", None, None), P("rep", None, "shard"))
    return jax.shard_map(
        local,
        mesh=mesh,
        in_specs=placed,
        out_specs=(P("rep", None, "shard"), P(None, "shard")),
        check_vma=False,
    )
```

```python
import functools

import jax
import jax.numpy as jnp
import numpy as np
from jax import lax
from jax.experimental import pallas as pl
from jax.experimental.pallas import tpu as pltpu
from jax.sharding import PartitionSpec as P

BETA = 0.9
SHARP = 4.0
ROWS = 256
LANES = 128
SUPER = 43
NB = 8
NBP = 4
MIDDLE = 21 - NB
NA = 7
OWN_COLS = 2752
PACKED = 352

VMEM_BYTES = 60 << 20

F32 = jnp.float32
BF16 = jnp.bfloat16


def x_shift(step):
    return [(s, ((s // 2 + step) % 4) * 2 + s % 2) for s in range(8)]


def z_shift(step):
    return [(r, (r // 8) * 8 + ((r // 2 % 4 + step) % 4) * 2 + r % 2) for r in range(16)]


def y_shift(step):
    pairs = []
    for r in range(16):
        for s in range(8):
            y = ((s % 2) * 2 + r // 8 + step) % 4
            pairs.append((r * 8 + s, ((y % 2) * 8 + r % 8) * 8 + (s // 2) * 2 + y // 2))
    return pairs


Y_FLIP = [(s, s ^ 1) for s in range(8)]
CORE_FLIP = [(r, r ^ 1) for r in range(16)]
Z_PAIR = [(r, r ^ 2) for r in range(16)]
Z_SKIP = [(r, r ^ 4) for r in range(16)]
YLO_FLIP = [(r, r ^ 8) for r in range(16)]


def send(name, value, axes, pairs):
    with jax.named_scope(name):
        return lax.ppermute(value, axes, pairs)


def up(name, value):
    return send(name + "_up", value, "shard", x_shift(1))


def down(name, value):
    return send(name + "_down", value, "shard", x_shift(-1))


def across(name, value):
    return send(name + "_across", value, "shard", Y_FLIP)


def dot(a, b, dims=((1,), (0,))):
    return lax.dot_general(a, b, (dims, ((), ())), preferred_element_type=F32)


def halves(value):
    high = value.astype(BF16)
    return high, (value - high.astype(F32)).astype(BF16)


def dot3(a, b, dims=((1,), (0,))):
    return dot(a[0], b[0], dims) + (dot(a[1], b[0], dims) + dot(a[0], b[1], dims))


def cosine_table():
    freqs = np.arange(16, dtype=np.float64)[:, None]
    points = np.arange(64, dtype=np.float64)[None, :]
    norming = np.where(freqs == 0.0, np.sqrt(1.0 / 64.0), np.sqrt(2.0 / 64.0))
    return norming * np.cos(np.pi * (2.0 * points + 1.0) * freqs / 128.0)


def table_parts():
    blocks = np.kron(np.eye(4), cosine_table())
    high = blocks.astype(jnp.bfloat16)
    low = (blocks - high.astype(np.float64)).astype(jnp.bfloat16)
    back = np.concatenate([high.T, high.T, low.T, np.zeros_like(high.T)], 1)
    return jnp.asarray(np.concatenate([high, low, back], 0))


def forward_t(whole, table):
    n = whole.shape[0]
    high, low = halves(whole)
    both = dot(high, table[:128], ((1,), (1,)))
    rowwise = both[:, :64] + (both[:, 64:] + dot(low, table[:64], ((1,), (1,))))
    out = []
    for at in range(0, n, 256):
        m = min(256, n - at)
        k = m // 4
        sides = jnp.concatenate(halves(rowwise[at : at + m, :]), 1)
        parts = table[:128] if m == 256 else jnp.concatenate([table[:k, :m], table[64 : 64 + k, :m]], 0)
        four = dot(parts, sides)
        out.append(four[:k, :64] + (four[k:, :64] + four[:k, 64:]))
    return out


def backward_t(coeffs, table):
    high, low = halves(coeffs)
    twice = jnp.concatenate([table[:64], table[:64]], 0)
    columns_of = dot(jnp.concatenate([high, low], 1), twice) + dot(high, table[64:128])
    out = []
    for at in range(0, coeffs.shape[0], 64):
        k = min(64, coeffs.shape[0] - at)
        high, low = halves(columns_of[at : at + k, :])
        if k == 64:
            out.append(dot(table[128:, :192], jnp.concatenate([high, low, high], 0)))
        else:
            out.append(dot3((table[:k, : 4 * k], table[64 : 64 + k, : 4 * k]), (high, low), ((0,), (0,))))
    return out


STEP = 128


def grads_block(rows, dx, tile, by_side, tiles):
    def where(row, place):
        first = ((place[0] + dx % 4) & 3) * SUPER + tile + by_side * place[1]
        return row * rows, pl.multiple_of(first * LANES, LANES)

    return pl.BlockSpec((pl.Element(rows), pl.Element(tiles * LANES)), where)


def columns(ref, first, tiles):
    return ref[:, first * LANES : (first + tiles) * LANES]


def step_kernel(body, n_ins, n_after, place, *refs):
    outs = refs[n_ins + n_after :]
    body(place, refs[:n_ins], outs[:-1])
    outs[-1][...] = jnp.zeros((8, LANES), F32)


class Steps:
    def __init__(self, place, grads):
        self.place, self.grads, self.mark = place, grads, []

    def __call__(self, name, body, slices, ins, out_tiles, after=()):
        after = [*self.mark, *after]
        with jax.named_scope(name):
            *outs, mark = pl.pallas_call(
                functools.partial(step_kernel, body, len(slices) + len(ins), len(after)),
                grid_spec=pltpu.PrefetchScalarGridSpec(
                    num_scalar_prefetch=1,
                    grid=(ROWS // STEP,),
                    in_specs=[grads_block(STEP, *piece) for piece in slices]
                    + [pl.BlockSpec((STEP, a.shape[1]), lambda r, _: (r, 0)) for a in ins]
                    + [pl.BlockSpec(memory_space=pl.ANY) for _ in after],
                    out_specs=[
                        pl.BlockSpec((STEP, t * LANES), lambda r, _: (r, 0)) for t in out_tiles
                    ]
                    + [pl.BlockSpec((8, LANES), lambda r, _: (0, 0))],
                ),
                out_shape=[jax.ShapeDtypeStruct((ROWS, t * LANES), F32) for t in out_tiles]
                + [jax.ShapeDtypeStruct((8, LANES), F32)],
                compiler_params=pltpu.CompilerParams(vmem_limit_bytes=VMEM_BYTES),
                cost_estimate=pl.CostEstimate(flops=0, bytes_accessed=1, transcendentals=0),
            )(self.place, *[self.grads] * len(slices), *ins, *after)
        self.mark = [mark]
        return outs


def read_body(place, ins, outs):
    ins = list(ins)
    for out in outs:
        at = 0
        while at < out.shape[1]:
            ref = ins.pop(0)
            out[:, at : at + ref.shape[1]] = ref[...].astype(F32)
            at += ref.shape[1]


def later_body(place, ins, outs):
    up_grads, down_grads, plus, minus = ins
    outs[0][...] = plus[...] + up_grads[...].astype(F32)
    outs[1][...] = minus[...] + down_grads[...].astype(F32)


def later_body(place, ins, outs):
    up_grads, down_grads, plus, minus = ins
    outs[0][...] = plus[...] + up_grads[...].astype(F32)
    outs[1][...] = minus[...] + down_grads[...].astype(F32)


def outer_body(first, place, ins, outs):
    up_grads, down_grads, came = ins[:3]
    ahead = columns(came, first, NBP) + up_grads[...].astype(F32)
    behind = columns(came, first + NBP, NB - NBP) + down_grads[...].astype(F32)
    if len(ins) > 3:
        ahead, behind = ahead + ins[3][...], behind + ins[4][...]
    outs[0][...] = ahead
    outs[1][...] = behind


def mix_a_body(place, ins, outs):
    g, plus, minus = ins

    @pl.when(place[1] == 0)
    def _():
        outs[0][...] = minus[...] + g[...].astype(F32)

    @pl.when(place[1] == 1)
    def _():
        w = NA * LANES
        outs[0][:, :w] = plus[...] + g[:, :w].astype(F32)
        outs[0][:, w:] = minus[:, :LANES] + g[:, w:].astype(F32)


def mix_b_body(place, ins, outs):
    g, plus, minus = ins

    @pl.when(place[1] == 0)
    def _():
        outs[0][...] = minus[...] + g[...].astype(F32)

    @pl.when(place[1] == 1)
    def _():
        outs[0][...] = plus[...] + g[...].astype(F32)


def pack(chunks):
    whole = jnp.concatenate(chunks, 0) if len(chunks) > 1 else chunks[0]
    n = whole.shape[0] // 2
    return jnp.concatenate([whole[:n], whole[n:]], 1)


def unpack(packed):
    return jnp.concatenate([packed[:, :64], packed[:, 64:]], 0)


def merge_kernel(plans, cols, n_before, n_ins, n_after, skips, place, *refs):
    momentum, table = refs[n_before : n_before + 2]
    ins = refs[n_before + 2 : n_before + 2 + n_ins]
    out, coeffs, mark, merged = refs[-4:]
    grads = refs[n_before + 2 + n_ins]
    for side, plan in enumerate(plans):

        @pl.when(place[1] == side)
        def _():
            for t, sources in enumerate(plan):
                total = columns(grads, t, 1).astype(F32)
                for ref, k in sources:
                    total = total + columns(ins[ref], k, 1)
                merged[t * LANES : (t + 1) * LANES, :] = total.T

    skip = pl.multiple_of(place[1] * 64, 64) if skips else 0
    whole = BETA * momentum[...] + merged[pl.ds(skip, cols), :]
    out[...] = whole
    coeffs[...] = pack(forward_t(whole, table[...]))
    mark[...] = jnp.zeros((8, LANES), F32)


def merge_call(name, steps, buffers, momentum_t, table, piece, first, row, cols, plans, ins):
    def rows(_, place):
        return pl.multiple_of(first[0] + (first[1] - first[0]) * place[1], 64), 0

    whole = lambda shape: pl.BlockSpec(shape, lambda i, _: (0, 0))
    part = pl.BlockSpec((pl.Element(cols), pl.Element(ROWS)), rows)
    packed = pl.BlockSpec((pl.Element(cols // 8), pl.Element(LANES)), lambda i, _: (row, 0))
    anywhere = lambda values: [pl.BlockSpec(memory_space=pl.ANY) for _ in values]
    tiles = piece[3]
    shapes = [(OWN_COLS, ROWS), (PACKED, LANES), (8, LANES)]
    with jax.named_scope(name):
        *buffers, mark = pl.pallas_call(
            functools.partial(
                merge_kernel, plans, cols, len(buffers), len(ins), len(steps.mark),
                cols < tiles * LANES,
            ),
            grid_spec=pltpu.PrefetchScalarGridSpec(
                num_scalar_prefetch=1,
                grid=(1,),
                in_specs=anywhere(buffers)
                + [part, whole(table.shape)]
                + [whole(a.shape) for a in ins]
                + [grads_block(ROWS, *piece)]
                + anywhere(steps.mark),
                out_specs=[part, packed, whole((8, LANES))],
                scratch_shapes=[pltpu.VMEM((tiles * LANES, ROWS), F32)],
            ),
            out_shape=[jax.ShapeDtypeStruct(shape, F32) for shape in shapes],
            input_output_aliases={1 + k: k for k in range(len(buffers))},
            compiler_params=pltpu.CompilerParams(vmem_limit_bytes=VMEM_BYTES),
            cost_estimate=pl.CostEstimate(flops=0, bytes_accessed=1, transcendentals=0),
        )(steps.place, *buffers, momentum_t, table, *ins, steps.grads, *steps.mark)
    steps.mark = [mark]
    return buffers


def groups_of(coeffs, groups):
    return [(g, unpack(coeffs[row : row + cols // 8, :])) for g, (_, row, cols) in enumerate(groups)]


def new_kernel(groups, place, whole, coeffs, table, out):
    for side in range(2):

        @pl.when(place[1] == side)
        def _():
            for g, chunks in groups_of(coeffs, groups):
                to = groups[g][0][side]
                for back in backward_t(chunks, table[...]):
                    end = to + back.shape[0]
                    out[to:end, :] = whole[to:end, :] - back
                    to = end


def update_kernel(groups, place, mine, other, table, out, coeffs):
    half = PACKED // 2
    coeffs[pl.ds(pl.multiple_of(place[3] * half, 8), half), :] = mine[...]
    coeffs[pl.ds(pl.multiple_of((1 - place[3]) * half, 8), half), :] = other[...]
    for side in range(2):

        @pl.when(place[1] == side)
        def _():
            for g, chunks in groups_of(coeffs, groups):
                to = groups[g][0][side]
                for back in backward_t(chunks, table[...]):
                    out[to : to + back.shape[0], :] = jnp.tanh((SHARP / 16.0) * back)
                    to += back.shape[0]


def output_call(name, kernel, place, ins, scratch):
    whole = lambda a: pl.BlockSpec(a.shape, lambda i, _: (0, 0))
    with jax.named_scope(name):
        return pl.pallas_call(
            kernel,
            grid_spec=pltpu.PrefetchScalarGridSpec(
                num_scalar_prefetch=1,
                grid=(1,),
                in_specs=[whole(a) for a in ins],
                out_specs=pl.BlockSpec((OWN_COLS, ROWS), lambda i, _: (0, 0)),
                scratch_shapes=scratch,
            ),
            out_shape=jax.ShapeDtypeStruct((OWN_COLS, ROWS), F32),
            compiler_params=pltpu.CompilerParams(vmem_limit_bytes=VMEM_BYTES),
            cost_estimate=pl.CostEstimate(flops=0, bytes_accessed=1, transcendentals=0),
        )(place, *ins)


def total_kernel(n, *refs):
    total = refs[0][...]
    for ref in refs[1:n]:
        total = total + ref[...]
    refs[-1][...] = total


def total_call(name, values, after):
    whole = lambda a: pl.BlockSpec(a.shape, lambda: (0, 0))
    with jax.named_scope(name):
        return pl.pallas_call(
            functools.partial(total_kernel, len(values)),
            in_specs=[whole(v) for v in values] + [pl.BlockSpec(memory_space=pl.ANY) for _ in after],
            out_specs=whole(values[0]),
            out_shape=jax.ShapeDtypeStruct(values[0].shape, F32),
            cost_estimate=pl.CostEstimate(flops=0, bytes_accessed=1, transcendentals=0),
        )(*values, *after)


def local(grads, momentum):
    grads = grads[0, 0]
    momentum_t = momentum[0].T
    shard = lax.axis_index("shard")
    x, yh = shard // 2, shard % 2
    table = table_parts()
    core = lax.axis_index("rep") % 2
    place = jnp.stack([x, yh, shard, core]).astype(jnp.int32)
    steps = Steps(place, grads)
    pairs = [[2 * k, 2 * k + 1] for k in range(4)]

    tiles_up, tiles_down = (21 - NA, NB), (21, 22 + NA)
    counts_up, counts_down = (NA, MIDDLE - NA), (NA + 1, MIDDLE - NA)

    def around(step, which, pair, after=()):
        name = "ab"[which] + str(step)
        slices = [
            (-1 - step, tiles_up[which], 0, counts_up[which]),
            (1 + step, tiles_down[which], 0, counts_down[which]),
        ]
        out = [counts_up[which], counts_down[which]]
        plus, minus = steps("add_" + name, later_body, slices, pair, out, after)
        return up(name, plus), down(name, minus)

    def cross(rounds):
        name = "cross" + "".join(map(str, rounds))
        slices = []
        for n in rounds:
            slices += [
                (-1 - n, SUPER - NB, NB - SUPER, NBP),
                (1 + n, SUPER - NB + NBP, NB - SUPER, NB - NBP),
            ]
        sent = steps("read_" + name, read_body, slices, [], [len(rounds) * NB])
        return across(name, sent[0])

    def outer(k, came, pair=(), after=()):
        slices = [(-1 - k, 0, SUPER - NB, NBP), (1 + k, NBP, SUPER - NB, NB - NBP)]
        body = functools.partial(outer_body, k % 2 * NB)
        plus, minus = steps(
            f"add_outer{k}", body, slices, [came, *pair], [NBP, NB - NBP], after
        )
        return up(f"outer{k}", plus), down(f"outer{k}", minus)

    slices, out = [], []
    for which in range(2):
        slices += [
            (-1, tiles_up[which], 0, counts_up[which]),
            (1, tiles_down[which], 0, counts_down[which]),
        ]
        out += [counts_up[which], counts_down[which]]
    plus_a, minus_a, plus_b, minus_b = steps("read_first", read_body, slices, [], out)
    a = up("a0", plus_a), down("a0", minus_a)
    b = up("b0", plus_b), down("b0", minus_b)
    y01 = cross((0, 1))
    y23 = cross((2, 3))
    a = around(1, 0, a)
    b = around(1, 1, b)
    o = outer(0, y01, after=a)
    a = around(2, 0, a, after=b)
    b = around(2, 1, b, after=o)
    ca = across("a", steps("mix_a", mix_a_body, [(0, 21, -NA, NA + 1)], a, [NA + 1])[0])
    o = outer(1, y01, o, after=a)
    mixed = steps(
        "mix_b", mix_b_body, [(0, 22 + NA, NB - 22 - NA, MIDDLE - NA)], b, [MIDDLE - NA]
    )
    cb = across("b", mixed[0])
    o = outer(2, y23, o, after=b)
    near, far = NA * LANES + 64, (MIDDLE - NA) * LANES
    groups = [
        (((21 - NA) * LANES, 0), 0, near),
        ((NB * LANES, near), near // 8, far),
        ((0, (SUPER - NB) * LANES - OWN_COLS), (near + far) // 8, NB * LANES),
    ]
    wide = lambda n, *refs: [[(r, t) for r in refs] for t in range(n)]
    buffers = merge_call(
        "merge_a", steps, [], momentum_t, table, (0, 21 - NA, NA, NA + 1), *groups[0],
        (wide(NA, 0, 2) + [[(1, 0), (2, NA)]], wide(NA + 1, 1, 2)), [*a, ca],
    )
    buffers = merge_call(
        "merge_b", steps, buffers, momentum_t, table, (0, NB, 22 + NA - NB, MIDDLE - NA),
        *groups[1], (wide(MIDDLE - NA, 0, 2), wide(MIDDLE - NA, 1, 2)), [*b, cb],
    )
    plan = [[(0, NB + t), (1, t) if t < NBP else (2, t - NBP)] for t in range(NB)]
    whole, coeffs = merge_call(
        "merge_outer", steps, buffers, momentum_t, table, (0, 0, SUPER - NB, NB), *groups[2],
        (plan, plan), [y23, *o],
    )
    half = PACKED // 2
    part = lambda c: lax.dynamic_slice(coeffs, (c * half, 0), (half, LANES))
    mine = part(core) + send("sum_core", part(1 - core), "rep", CORE_FLIP)
    came = [send(f"sum_z{k}", mine, "rep", z_shift(k)) for k in (2, 1, 3)]
    new_t = output_call(
        "new_momentum", functools.partial(new_kernel, groups), place, [whole, coeffs, table], []
    )
    mine = total_call("sum_z", [mine, *came], [new_t])
    mine = mine + send("sum_y", mine, "rep", YLO_FLIP)
    other = send("gather_core", mine, "rep", CORE_FLIP)
    update_t = output_call(
        "update", functools.partial(update_kernel, groups), place, [mine, other, table],
        [pltpu.VMEM((PACKED, LANES), F32)],
    )
    return new_t.T[None], update_t.T


def solution(mesh):
    placed = (P("rep", "shard", None, None), P("rep", None, "shard"))
    return jax.shard_map(
        local,
        mesh=mesh,
        in_specs=placed,
        out_specs=(P("rep", None, "shard"), P(None, "shard")),
        check_vma=False,
    )
```

```python
import functools

import jax
import jax.numpy as jnp
import numpy as np
from jax import lax
from jax.experimental import pallas as pl
from jax.experimental.pallas import tpu as pltpu
from jax.sharding import PartitionSpec as P

BETA = 0.9
SHARP = 4.0
ROWS = 256
LANES = 128
SUPER = 43
NB = 9
NBP = 5
MIDDLE = 21 - NB
NA = 6
OWN_COLS = 2752
PACKED = 352

VMEM_BYTES = 60 << 20

F32 = jnp.float32
BF16 = jnp.bfloat16


def x_shift(step):
    return [(s, ((s // 2 + step) % 4) * 2 + s % 2) for s in range(8)]


def z_shift(step):
    return [(r, (r // 8) * 8 + ((r // 2 % 4 + step) % 4) * 2 + r % 2) for r in range(16)]


def y_shift(step):
    pairs = []
    for r in range(16):
        for s in range(8):
            y = ((s % 2) * 2 + r // 8 + step) % 4
            pairs.append((r * 8 + s, ((y % 2) * 8 + r % 8) * 8 + (s // 2) * 2 + y // 2))
    return pairs


Y_FLIP = [(s, s ^ 1) for s in range(8)]
CORE_FLIP = [(r, r ^ 1) for r in range(16)]
Z_PAIR = [(r, r ^ 2) for r in range(16)]
Z_SKIP = [(r, r ^ 4) for r in range(16)]
YLO_FLIP = [(r, r ^ 8) for r in range(16)]


def send(name, value, axes, pairs):
    with jax.named_scope(name):
        return lax.ppermute(value, axes, pairs)


def up(name, value):
    return send(name + "_up", value, "shard", x_shift(1))


def down(name, value):
    return send(name + "_down", value, "shard", x_shift(-1))


def across(name, value):
    return send(name + "_across", value, "shard", Y_FLIP)


def dot(a, b, dims=((1,), (0,))):
    return lax.dot_general(a, b, (dims, ((), ())), preferred_element_type=F32)


def halves(value):
    high = value.astype(BF16)
    return high, (value - high.astype(F32)).astype(BF16)


def dot3(a, b, dims=((1,), (0,))):
    return dot(a[0], b[0], dims) + (dot(a[1], b[0], dims) + dot(a[0], b[1], dims))


def cosine_table():
    freqs = np.arange(16, dtype=np.float64)[:, None]
    points = np.arange(64, dtype=np.float64)[None, :]
    norming = np.where(freqs == 0.0, np.sqrt(1.0 / 64.0), np.sqrt(2.0 / 64.0))
    return norming * np.cos(np.pi * (2.0 * points + 1.0) * freqs / 128.0)


def table_parts():
    blocks = np.kron(np.eye(4), cosine_table())
    high = blocks.astype(jnp.bfloat16)
    low = (blocks - high.astype(np.float64)).astype(jnp.bfloat16)
    back = np.concatenate([high.T, high.T, low.T, np.zeros_like(high.T)], 1)
    return jnp.asarray(np.concatenate([high, low, back], 0))


def forward_t(whole, table):
    n = whole.shape[0]
    high, low = halves(whole)
    both = dot(high, table[:128], ((1,), (1,)))
    rowwise = both[:, :64] + (both[:, 64:] + dot(low, table[:64], ((1,), (1,))))
    out = []
    for at in range(0, n, 256):
        m = min(256, n - at)
        k = m // 4
        sides = jnp.concatenate(halves(rowwise[at : at + m, :]), 1)
        parts = table[:128] if m == 256 else jnp.concatenate([table[:k, :m], table[64 : 64 + k, :m]], 0)
        four = dot(parts, sides)
        out.append(four[:k, :64] + (four[k:, :64] + four[:k, 64:]))
    return out


def backward_t(coeffs, table):
    high, low = halves(coeffs)
    twice = jnp.concatenate([table[:64], table[:64]], 0)
    columns_of = dot(jnp.concatenate([high, low], 1), twice) + dot(high, table[64:128])
    out = []
    for at in range(0, coeffs.shape[0], 64):
        k = min(64, coeffs.shape[0] - at)
        high, low = halves(columns_of[at : at + k, :])
        if k == 64:
            out.append(dot(table[128:, :192], jnp.concatenate([high, low, high], 0)))
        else:
            out.append(dot3((table[:k, : 4 * k], table[64 : 64 + k, : 4 * k]), (high, low), ((0,), (0,))))
    return out


STEP = 128


def grads_block(rows, dx, tile, by_side, tiles):
    def where(row, place):
        first = ((place[0] + dx % 4) & 3) * SUPER + tile + by_side * place[1]
        return row * rows, pl.multiple_of(first * LANES, LANES)

    return pl.BlockSpec((pl.Element(rows), pl.Element(tiles * LANES)), where)


def columns(ref, first, tiles):
    return ref[:, first * LANES : (first + tiles) * LANES]


def step_kernel(body, n_ins, n_after, place, *refs):
    outs = refs[n_ins + n_after :]
    body(place, refs[:n_ins], outs[:-1])
    outs[-1][...] = jnp.zeros((8, LANES), F32)


class Steps:
    def __init__(self, place, grads):
        self.place, self.grads, self.mark = place, grads, []

    def __call__(self, name, body, slices, ins, out_tiles, after=()):
        after = [*self.mark, *after]
        with jax.named_scope(name):
            *outs, mark = pl.pallas_call(
                functools.partial(step_kernel, body, len(slices) + len(ins), len(after)),
                grid_spec=pltpu.PrefetchScalarGridSpec(
                    num_scalar_prefetch=1,
                    grid=(ROWS // STEP,),
                    in_specs=[grads_block(STEP, *piece) for piece in slices]
                    + [pl.BlockSpec((STEP, a.shape[1]), lambda r, _: (r, 0)) for a in ins]
                    + [pl.BlockSpec(memory_space=pl.ANY) for _ in after],
                    out_specs=[
                        pl.BlockSpec((STEP, t * LANES), lambda r, _: (r, 0)) for t in out_tiles
                    ]
                    + [pl.BlockSpec((8, LANES), lambda r, _: (0, 0))],
                ),
                out_shape=[jax.ShapeDtypeStruct((ROWS, t * LANES), F32) for t in out_tiles]
                + [jax.ShapeDtypeStruct((8, LANES), F32)],
                compiler_params=pltpu.CompilerParams(vmem_limit_bytes=VMEM_BYTES),
                cost_estimate=pl.CostEstimate(flops=0, bytes_accessed=1, transcendentals=0),
            )(self.place, *[self.grads] * len(slices), *ins, *after)
        self.mark = [mark]
        return outs


def read_body(place, ins, outs):
    ins = list(ins)
    for out in outs:
        at = 0
        while at < out.shape[1]:
            ref = ins.pop(0)
            out[:, at : at + ref.shape[1]] = ref[...].astype(F32)
            at += ref.shape[1]


def later_body(place, ins, outs):
    up_grads, down_grads, plus, minus = ins
    outs[0][...] = plus[...] + up_grads[...].astype(F32)
    outs[1][...] = minus[...] + down_grads[...].astype(F32)


def later_body(place, ins, outs):
    up_grads, down_grads, plus, minus = ins
    outs[0][...] = plus[...] + up_grads[...].astype(F32)
    outs[1][...] = minus[...] + down_grads[...].astype(F32)


def outer_body(first, place, ins, outs):
    up_grads, down_grads, came = ins[:3]
    ahead = columns(came, first, NBP) + up_grads[...].astype(F32)
    behind = columns(came, first + NBP, NB - NBP) + down_grads[...].astype(F32)
    if len(ins) > 3:
        ahead, behind = ahead + ins[3][...], behind + ins[4][...]
    outs[0][...] = ahead
    outs[1][...] = behind


def mix_a_body(place, ins, outs):
    g, plus, minus = ins

    @pl.when(place[1] == 0)
    def _():
        outs[0][...] = minus[...] + g[...].astype(F32)

    @pl.when(place[1] == 1)
    def _():
        w = NA * LANES
        outs[0][:, :w] = plus[...] + g[:, :w].astype(F32)
        outs[0][:, w:] = minus[:, :LANES] + g[:, w:].astype(F32)


def mix_b_body(place, ins, outs):
    g, plus, minus = ins

    @pl.when(place[1] == 0)
    def _():
        outs[0][...] = minus[...] + g[...].astype(F32)

    @pl.when(place[1] == 1)
    def _():
        outs[0][...] = plus[...] + g[...].astype(F32)


def pack(chunks):
    whole = jnp.concatenate(chunks, 0) if len(chunks) > 1 else chunks[0]
    n = whole.shape[0] // 2
    return jnp.concatenate([whole[:n], whole[n:]], 1)


def unpack(packed):
    return jnp.concatenate([packed[:, :64], packed[:, 64:]], 0)


def merge_kernel(groups, n_before, final, place, *refs):
    refs = list(refs[n_before:])
    table, coeffs, mark, merged = refs.pop(0), refs[-3], refs[-2], refs[-1]
    row = 0
    for g, (n_ins, cols, tiles, skips, plans) in enumerate(groups):
        momentum, grads, *ins = refs[: 2 + n_ins]
        del refs[: 2 + n_ins]
        out = refs[len(refs) - 3 - len(groups) + g]
        for side, plan in enumerate(plans):

            @pl.when(place[1] == side)
            def _():
                for t, sources in enumerate(plan):
                    total = columns(grads, t, 1).astype(F32)
                    for ref, k in sources:
                        total = total + columns(ins[ref], k, 1)
                    merged[t * LANES : (t + 1) * LANES, :] = total.T

        skip = pl.multiple_of(place[1] * 64, 64) if skips else 0
        whole = BETA * momentum[...] + merged[pl.ds(skip, cols), :]
        chunks = forward_t(whole, table[...])
        coeffs[row : row + cols // 8, :] = pack(chunks)
        if final:
            at = 0
            for back in backward_t(jnp.concatenate(chunks, 0), table[...]):
                end = at + back.shape[0]
                out[at:end, :] = whole[at:end] - back
                at = end
        else:
            out[...] = whole
        row += cols // 8
    mark[...] = jnp.zeros((8, LANES), F32)


def merge_call(name, steps, before, momentum_t, table, row, groups, final=False):
    whole = lambda shape: pl.BlockSpec(shape, lambda i, _: (0, 0))

    def part(first, cols):
        def rows(_, place):
            return pl.multiple_of(first[0] + (first[1] - first[0]) * place[1], 64), 0

        return pl.BlockSpec((pl.Element(cols), pl.Element(ROWS)), rows)

    before = [*before, *steps.mark]
    aliases = {1: len(groups)} if len(before) > len(steps.mark) else {}
    anywhere = [pl.BlockSpec(memory_space=pl.ANY) for _ in before]
    in_specs, ins, counts = [], [], []
    for piece, first, cols, plans, values in groups:
        in_specs += [part(first, cols), grads_block(ROWS, *piece), *[whole(v.shape) for v in values]]
        ins += [momentum_t, steps.grads, *values]
        counts.append((len(values), cols, piece[3], cols < piece[3] * LANES, plans))
    rows = sum(group[2] for group in groups) // 8
    packed = pl.BlockSpec((pl.Element(rows), pl.Element(LANES)), lambda i, _: (row, 0))
    shapes = [(group[2], ROWS) for group in groups]
    tiles = max(group[0][3] for group in groups)
    with jax.named_scope(name):
        *wholes, coeffs, mark = pl.pallas_call(
            functools.partial(merge_kernel, counts, len(before), final),
            grid_spec=pltpu.PrefetchScalarGridSpec(
                num_scalar_prefetch=1,
                grid=(1,),
                in_specs=anywhere + [whole(table.shape)] + in_specs,
                out_specs=[whole(shape) for shape in shapes] + [packed, whole((8, LANES))],
                scratch_shapes=[pltpu.VMEM((tiles * LANES, ROWS), F32)],
            ),
            out_shape=[
                jax.ShapeDtypeStruct(shape, F32)
                for shape in [*shapes, (PACKED, LANES), (8, LANES)]
            ],
            input_output_aliases=aliases,
            compiler_params=pltpu.CompilerParams(vmem_limit_bytes=VMEM_BYTES),
            cost_estimate=pl.CostEstimate(flops=0, bytes_accessed=1, transcendentals=0),
        )(steps.place, *before, table, *ins)
    steps.mark = [mark]
    return wholes, coeffs


def groups_of(coeffs, groups):
    return [(g, unpack(coeffs[row : row + cols // 8, :])) for g, (_, row, cols) in enumerate(groups)]


def new_kernel(groups, place, *refs):
    *wholes, coeffs, table, out = refs
    for side in range(2):

        @pl.when(place[1] == side)
        def _():
            for g, chunks in groups_of(coeffs, groups):
                to, n = groups[g][0][side], groups[g][2]
                if g == 0:
                    out[to : to + n, :] = wholes[0][...]
                    continue
                at = 0
                for back in backward_t(chunks, table[...]):
                    n = back.shape[0]
                    out[to + at : to + at + n, :] = wholes[g][at : at + n, :] - back
                    at += n


def update_kernel(groups, place, mine, other, table, out, coeffs):
    half = PACKED // 2
    coeffs[pl.ds(pl.multiple_of(place[3] * half, 8), half), :] = mine[...]
    coeffs[pl.ds(pl.multiple_of((1 - place[3]) * half, 8), half), :] = other[...]
    for side in range(2):

        @pl.when(place[1] == side)
        def _():
            for g, chunks in groups_of(coeffs, groups):
                to = groups[g][0][side]
                for back in backward_t(chunks, table[...]):
                    out[to : to + back.shape[0], :] = jnp.tanh((SHARP / 16.0) * back)
                    to += back.shape[0]


def output_call(name, kernel, place, ins, scratch):
    whole = lambda a: pl.BlockSpec(a.shape, lambda i, _: (0, 0))
    with jax.named_scope(name):
        return pl.pallas_call(
            kernel,
            grid_spec=pltpu.PrefetchScalarGridSpec(
                num_scalar_prefetch=1,
                grid=(1,),
                in_specs=[whole(a) for a in ins],
                out_specs=pl.BlockSpec((OWN_COLS, ROWS), lambda i, _: (0, 0)),
                scratch_shapes=scratch,
            ),
            out_shape=jax.ShapeDtypeStruct((OWN_COLS, ROWS), F32),
            compiler_params=pltpu.CompilerParams(vmem_limit_bytes=VMEM_BYTES),
            cost_estimate=pl.CostEstimate(flops=0, bytes_accessed=1, transcendentals=0),
        )(place, *ins)


def total_kernel(n, *refs):
    total = refs[0][...]
    for ref in refs[1:n]:
        total = total + ref[...]
    refs[-1][...] = total


def total_call(name, values, after):
    whole = lambda a: pl.BlockSpec(a.shape, lambda: (0, 0))
    with jax.named_scope(name):
        return pl.pallas_call(
            functools.partial(total_kernel, len(values)),
            in_specs=[whole(v) for v in values] + [pl.BlockSpec(memory_space=pl.ANY) for _ in after],
            out_specs=whole(values[0]),
            out_shape=jax.ShapeDtypeStruct(values[0].shape, F32),
            cost_estimate=pl.CostEstimate(flops=0, bytes_accessed=1, transcendentals=0),
        )(*values, *after)


def local(grads, momentum):
    grads = grads[0, 0]
    momentum_t = momentum[0].T
    shard = lax.axis_index("shard")
    x, yh = shard // 2, shard % 2
    table = table_parts()
    core = lax.axis_index("rep") % 2
    place = jnp.stack([x, yh, shard, core]).astype(jnp.int32)
    steps = Steps(place, grads)
    pairs = [[2 * k, 2 * k + 1] for k in range(4)]

    tiles_up, tiles_down = (21 - NA, NB), (21, 22 + NA)
    counts_up, counts_down = (NA, MIDDLE - NA), (NA + 1, MIDDLE - NA)

    def around(step, which, pair, after=()):
        name = "ab"[which] + str(step)
        slices = [
            (-1 - step, tiles_up[which], 0, counts_up[which]),
            (1 + step, tiles_down[which], 0, counts_down[which]),
        ]
        out = [counts_up[which], counts_down[which]]
        plus, minus = steps("add_" + name, later_body, slices, pair, out, after)
        return up(name, plus), down(name, minus)

    def cross(rounds):
        name = "cross" + "".join(map(str, rounds))
        slices = []
        for n in rounds:
            slices += [
                (-1 - n, SUPER - NB, NB - SUPER, NBP),
                (1 + n, SUPER - NB + NBP, NB - SUPER, NB - NBP),
            ]
        sent = steps("read_" + name, read_body, slices, [], [len(rounds) * NB])
        return across(name, sent[0])

    def outer(k, came, pair=(), after=()):
        slices = [(-1 - k, 0, SUPER - NB, NBP), (1 + k, NBP, SUPER - NB, NB - NBP)]
        body = functools.partial(outer_body, k % 2 * NB)
        plus, minus = steps(
            f"add_outer{k}", body, slices, [came, *pair], [NBP, NB - NBP], after
        )
        return up(f"outer{k}", plus), down(f"outer{k}", minus)

    slices, out = [], []
    for which in range(2):
        slices += [
            (-1, tiles_up[which], 0, counts_up[which]),
            (1, tiles_down[which], 0, counts_down[which]),
        ]
        out += [counts_up[which], counts_down[which]]
    plus_a, minus_a, plus_b, minus_b = steps("read_first", read_body, slices, [], out)
    a = up("a0", plus_a), down("a0", minus_a)
    b = up("b0", plus_b), down("b0", minus_b)
    y01 = cross((0, 1))
    y23 = cross((2, 3))
    a = around(1, 0, a)
    b = around(1, 1, b)
    a = around(2, 0, a)
    o = outer(0, y01, after=b)
    b = around(2, 1, b, after=a)
    ca = across("a", steps("mix_a", mix_a_body, [(0, 21, -NA, NA + 1)], a, [NA + 1])[0])
    o = outer(1, y01, o, after=[y23])
    mixed = steps(
        "mix_b", mix_b_body, [(0, 22 + NA, NB - 22 - NA, MIDDLE - NA)], b, [MIDDLE - NA]
    )
    cb = across("b", mixed[0])
    o = outer(2, y23, o, after=b)

    near, far = NA * LANES + 64, (MIDDLE - NA) * LANES
    groups = [
        (((21 - NA) * LANES, 0), 0, near),
        ((NB * LANES, near), near // 8, far),
        ((0, (SUPER - NB) * LANES - OWN_COLS), (near + far) // 8, NB * LANES),
    ]
    wide = lambda n, *refs: [[(r, t) for r in refs] for t in range(n)]
    plan = [[(0, NB + t), (1, t) if t < NBP else (2, t - NBP)] for t in range(NB)]
    sides = (wide(NA, 0, 2) + [[(1, 0), (2, NA)]], wide(NA + 1, 1, 2))
    (whole_a,), coeffs = merge_call(
        "merge_a", steps, [], momentum_t, table, groups[0][1],
        [((0, 21 - NA, NA, NA + 1), groups[0][0], near, sides, [*a, ca])],
        final=True,
    )
    sides = (wide(MIDDLE - NA, 0, 2), wide(MIDDLE - NA, 1, 2))
    rest, coeffs = merge_call(
        "merge_rest", steps, [coeffs], momentum_t, table, groups[1][1],
        [
            ((0, NB, 22 + NA - NB, MIDDLE - NA), groups[1][0], far, sides, [*b, cb]),
            ((0, 0, SUPER - NB, NB), groups[2][0], NB * LANES, (plan, plan), [y23, *o]),
        ],
    )
    half = PACKED // 2
    part = lambda c: lax.dynamic_slice(coeffs, (c * half, 0), (half, LANES))
    mine = part(core) + send("sum_core", part(1 - core), "rep", CORE_FLIP)
    came = [send(f"sum_z{k}", mine, "rep", z_shift(k)) for k in (2, 1, 3)]
    new_t = output_call(
        "new_momentum", functools.partial(new_kernel, groups), place,
        [whole_a, *rest, coeffs, table], [],
    )
    mine = total_call("sum_z", [mine, *came], [new_t])
    mine = mine + send("sum_y", mine, "rep", YLO_FLIP)
    other = send("gather_core", mine, "rep", CORE_FLIP)
    update_t = output_call(
        "update", functools.partial(update_kernel, groups), place, [mine, other, table],
        [pltpu.VMEM((PACKED, LANES), F32)],
    )
    return new_t.T[None], update_t.T


def solution(mesh):
    placed = (P("rep", "shard", None, None), P("rep", None, "shard"))
    return jax.shard_map(
        local,
        mesh=mesh,
        in_specs=placed,
        out_specs=(P("rep", None, "shard"), P(None, "shard")),
        check_vma=False,
    )
```

```python
import functools

import jax
import jax.numpy as jnp
import numpy as np
from jax import lax
from jax.experimental import pallas as pl
from jax.experimental.pallas import tpu as pltpu
from jax.sharding import PartitionSpec as P

BETA = 0.9
SHARP = 4.0
ROWS = 256
LANES = 128
SUPER = 43
NB = 9
NBP = 5
MIDDLE = 21 - NB
NA = 6
OWN_COLS = 2752
PACKED = 352

VMEM_BYTES = 60 << 20

F32 = jnp.float32
BF16 = jnp.bfloat16


def x_shift(step):
    return [(s, ((s // 2 + step) % 4) * 2 + s % 2) for s in range(8)]


def z_shift(step):
    return [(r, (r // 8) * 8 + ((r // 2 % 4 + step) % 4) * 2 + r % 2) for r in range(16)]


def y_shift(step):
    pairs = []
    for r in range(16):
        for s in range(8):
            y = ((s % 2) * 2 + r // 8 + step) % 4
            pairs.append((r * 8 + s, ((y % 2) * 8 + r % 8) * 8 + (s // 2) * 2 + y // 2))
    return pairs


Y_FLIP = [(s, s ^ 1) for s in range(8)]
CORE_FLIP = [(r, r ^ 1) for r in range(16)]
Z_PAIR = [(r, r ^ 2) for r in range(16)]
Z_SKIP = [(r, r ^ 4) for r in range(16)]
YLO_FLIP = [(r, r ^ 8) for r in range(16)]


def send(name, value, axes, pairs):
    with jax.named_scope(name):
        return lax.ppermute(value, axes, pairs)


def up(name, value):
    return send(name + "_up", value, "shard", x_shift(1))


def down(name, value):
    return send(name + "_down", value, "shard", x_shift(-1))


def across(name, value):
    return send(name + "_across", value, "shard", Y_FLIP)


def dot(a, b, dims=((1,), (0,))):
    return lax.dot_general(a, b, (dims, ((), ())), preferred_element_type=F32)


def halves(value):
    high = value.astype(BF16)
    return high, (value - high.astype(F32)).astype(BF16)


def dot3(a, b, dims=((1,), (0,))):
    return dot(a[0], b[0], dims) + (dot(a[1], b[0], dims) + dot(a[0], b[1], dims))


def cosine_table():
    freqs = np.arange(16, dtype=np.float64)[:, None]
    points = np.arange(64, dtype=np.float64)[None, :]
    norming = np.where(freqs == 0.0, np.sqrt(1.0 / 64.0), np.sqrt(2.0 / 64.0))
    return norming * np.cos(np.pi * (2.0 * points + 1.0) * freqs / 128.0)


def table_parts():
    blocks = np.kron(np.eye(4), cosine_table())
    high = blocks.astype(jnp.bfloat16)
    low = (blocks - high.astype(np.float64)).astype(jnp.bfloat16)
    back = np.concatenate([high.T, high.T, low.T, np.zeros_like(high.T)], 1)
    return jnp.asarray(np.concatenate([high, low, back], 0))


def forward_t(whole, table):
    n = whole.shape[0]
    high, low = halves(whole)
    both = dot(high, table[:128], ((1,), (1,)))
    rowwise = both[:, :64] + (both[:, 64:] + dot(low, table[:64], ((1,), (1,))))
    out = []
    for at in range(0, n, 256):
        m = min(256, n - at)
        k = m // 4
        sides = jnp.concatenate(halves(rowwise[at : at + m, :]), 1)
        parts = table[:128] if m == 256 else jnp.concatenate([table[:k, :m], table[64 : 64 + k, :m]], 0)
        four = dot(parts, sides)
        out.append(four[:k, :64] + (four[k:, :64] + four[:k, 64:]))
    return out


def backward_t(coeffs, table):
    high, low = halves(coeffs)
    twice = jnp.concatenate([table[:64], table[:64]], 0)
    columns_of = dot(jnp.concatenate([high, low], 1), twice) + dot(high, table[64:128])
    out = []
    for at in range(0, coeffs.shape[0], 64):
        k = min(64, coeffs.shape[0] - at)
        high, low = halves(columns_of[at : at + k, :])
        if k == 64:
            out.append(dot(table[128:, :192], jnp.concatenate([high, low, high], 0)))
        else:
            out.append(dot3((table[:k, : 4 * k], table[64 : 64 + k, : 4 * k]), (high, low), ((0,), (0,))))
    return out


STEP = 128


def grads_block(rows, dx, tile, by_side, tiles):
    def where(row, place):
        first = ((place[0] + dx % 4) & 3) * SUPER + tile + by_side * place[1]
        return row * rows, pl.multiple_of(first * LANES, LANES)

    return pl.BlockSpec((pl.Element(rows), pl.Element(tiles * LANES)), where)


def columns(ref, first, tiles):
    return ref[:, first * LANES : (first + tiles) * LANES]


def step_kernel(body, n_ins, n_after, place, *refs):
    outs = refs[n_ins + n_after :]
    body(place, refs[:n_ins], outs[:-1])
    outs[-1][...] = jnp.zeros((8, LANES), F32)


class Steps:
    def __init__(self, place, grads):
        self.place, self.grads, self.mark = place, grads, []

    def __call__(self, name, body, slices, ins, out_tiles, after=()):
        after = [*self.mark, *after]
        with jax.named_scope(name):
            *outs, mark = pl.pallas_call(
                functools.partial(step_kernel, body, len(slices) + len(ins), len(after)),
                grid_spec=pltpu.PrefetchScalarGridSpec(
                    num_scalar_prefetch=1,
                    grid=(ROWS // STEP,),
                    in_specs=[grads_block(STEP, *piece) for piece in slices]
                    + [pl.BlockSpec((STEP, a.shape[1]), lambda r, _: (r, 0)) for a in ins]
                    + [pl.BlockSpec(memory_space=pl.ANY) for _ in after],
                    out_specs=[
                        pl.BlockSpec((STEP, t * LANES), lambda r, _: (r, 0)) for t in out_tiles
                    ]
                    + [pl.BlockSpec((8, LANES), lambda r, _: (0, 0))],
                ),
                out_shape=[jax.ShapeDtypeStruct((ROWS, t * LANES), F32) for t in out_tiles]
                + [jax.ShapeDtypeStruct((8, LANES), F32)],
                compiler_params=pltpu.CompilerParams(vmem_limit_bytes=VMEM_BYTES),
                cost_estimate=pl.CostEstimate(flops=0, bytes_accessed=1, transcendentals=0),
            )(self.place, *[self.grads] * len(slices), *ins, *after)
        self.mark = [mark]
        return outs


def read_body(place, ins, outs):
    ins = list(ins)
    for out in outs:
        at = 0
        while at < out.shape[1]:
            ref = ins.pop(0)
            out[:, at : at + ref.shape[1]] = ref[...].astype(F32)
            at += ref.shape[1]


def later_body(place, ins, outs):
    up_grads, down_grads, plus, minus = ins
    outs[0][...] = plus[...] + up_grads[...].astype(F32)
    outs[1][...] = minus[...] + down_grads[...].astype(F32)


def later_body(place, ins, outs):
    up_grads, down_grads, plus, minus = ins
    outs[0][...] = plus[...] + up_grads[...].astype(F32)
    outs[1][...] = minus[...] + down_grads[...].astype(F32)


def outer_body(first, place, ins, outs):
    up_grads, down_grads, came = ins[:3]
    ahead = columns(came, first, NBP) + up_grads[...].astype(F32)
    behind = columns(came, first + NBP, NB - NBP) + down_grads[...].astype(F32)
    if len(ins) > 3:
        ahead, behind = ahead + ins[3][...], behind + ins[4][...]
    outs[0][...] = ahead
    outs[1][...] = behind


def mix_a_body(place, ins, outs):
    g, plus, minus = ins

    @pl.when(place[1] == 0)
    def _():
        outs[0][...] = minus[...] + g[...].astype(F32)

    @pl.when(place[1] == 1)
    def _():
        w = NA * LANES
        outs[0][:, :w] = plus[...] + g[:, :w].astype(F32)
        outs[0][:, w:] = minus[:, :LANES] + g[:, w:].astype(F32)


def mix_b_body(place, ins, outs):
    g, plus, minus = ins

    @pl.when(place[1] == 0)
    def _():
        outs[0][...] = minus[...] + g[...].astype(F32)

    @pl.when(place[1] == 1)
    def _():
        outs[0][...] = plus[...] + g[...].astype(F32)


def pack(chunks):
    whole = jnp.concatenate(chunks, 0) if len(chunks) > 1 else chunks[0]
    n = whole.shape[0] // 2
    return jnp.concatenate([whole[:n], whole[n:]], 1)


def unpack(packed):
    return jnp.concatenate([packed[:, :64], packed[:, 64:]], 0)


def merge_kernel(groups, n_before, place, *refs):
    refs = list(refs[n_before:])
    table, (out, coeffs, mark, merged) = refs.pop(0), refs[-4:]
    row = 0
    for n_ins, cols, tiles, skips, starts, plans in groups:
        momentum, grads, *ins = refs[: 2 + n_ins]
        del refs[: 2 + n_ins]
        for side, plan in enumerate(plans):

            @pl.when(place[1] == side)
            def _():
                for t, sources in enumerate(plan):
                    total = columns(grads, t, 1).astype(F32)
                    for ref, k in sources:
                        total = total + columns(ins[ref], k, 1)
                    merged[t * LANES : (t + 1) * LANES, :] = total.T

        skip = pl.multiple_of(place[1] * 64, 64) if skips else 0
        whole = BETA * momentum[...] + merged[pl.ds(skip, cols), :]
        chunks = forward_t(whole, table[...])
        coeffs[row : row + cols // 8, :] = pack(chunks)
        start = pl.multiple_of(starts[0] + (starts[1] - starts[0]) * place[1], 64)
        at = 0
        for back in backward_t(jnp.concatenate(chunks, 0), table[...]):
            n = back.shape[0]
            out[pl.ds(start + at, n), :] = whole[at : at + n] - back
            at += n
        row += cols // 8
    mark[...] = jnp.zeros((8, LANES), F32)


def merge_call(name, steps, before, momentum_t, table, row, groups):
    whole = lambda shape: pl.BlockSpec(shape, lambda i, _: (0, 0))

    def part(first, cols):
        def rows(_, place):
            return pl.multiple_of(first[0] + (first[1] - first[0]) * place[1], 64), 0

        return pl.BlockSpec((pl.Element(cols), pl.Element(ROWS)), rows)

    before = [*before, *steps.mark]
    aliases = {1: 0, 2: 1} if len(before) > len(steps.mark) else {}
    anywhere = [pl.BlockSpec(memory_space=pl.ANY) for _ in before]
    least = tuple(min(group[1][side] for group in groups) for side in range(2))
    in_specs, ins, counts = [], [], []
    for piece, first, cols, plans, values in groups:
        in_specs += [part(first, cols), grads_block(ROWS, *piece), *[whole(v.shape) for v in values]]
        ins += [momentum_t, steps.grads, *values]
        starts = (first[0] - least[0], first[1] - least[1])
        counts.append((len(values), cols, piece[3], cols < piece[3] * LANES, starts, plans))
    rows = sum(group[2] for group in groups) // 8
    packed = pl.BlockSpec((pl.Element(rows), pl.Element(LANES)), lambda i, _: (row, 0))
    tiles = max(group[0][3] for group in groups)
    with jax.named_scope(name):
        out, coeffs, mark = pl.pallas_call(
            functools.partial(merge_kernel, counts, len(before)),
            grid_spec=pltpu.PrefetchScalarGridSpec(
                num_scalar_prefetch=1,
                grid=(1,),
                in_specs=anywhere + [whole(table.shape)] + in_specs,
                out_specs=[part(least, rows * 8), packed, whole((8, LANES))],
                scratch_shapes=[pltpu.VMEM((tiles * LANES, ROWS), F32)],
            ),
            out_shape=[
                jax.ShapeDtypeStruct(shape, F32)
                for shape in [(OWN_COLS, ROWS), (PACKED, LANES), (8, LANES)]
            ],
            input_output_aliases=aliases,
            compiler_params=pltpu.CompilerParams(vmem_limit_bytes=VMEM_BYTES),
            cost_estimate=pl.CostEstimate(flops=0, bytes_accessed=1, transcendentals=0),
        )(steps.place, *before, table, *ins)
    steps.mark = [mark]
    return out, coeffs


def groups_of(coeffs, groups):
    return [(g, unpack(coeffs[row : row + cols // 8, :])) for g, (_, row, cols) in enumerate(groups)]


def update_kernel(groups, place, mine, other, table, out, coeffs):
    half = PACKED // 2
    coeffs[pl.ds(pl.multiple_of(place[3] * half, 8), half), :] = mine[...]
    coeffs[pl.ds(pl.multiple_of((1 - place[3]) * half, 8), half), :] = other[...]
    for side in range(2):

        @pl.when(place[1] == side)
        def _():
            for g, chunks in groups_of(coeffs, groups):
                to = groups[g][0][side]
                for back in backward_t(chunks, table[...]):
                    out[to : to + back.shape[0], :] = jnp.tanh((SHARP / 16.0) * back)
                    to += back.shape[0]


def output_call(name, kernel, place, ins, scratch):
    whole = lambda a: pl.BlockSpec(a.shape, lambda i, _: (0, 0))
    with jax.named_scope(name):
        return pl.pallas_call(
            kernel,
            grid_spec=pltpu.PrefetchScalarGridSpec(
                num_scalar_prefetch=1,
                grid=(1,),
                in_specs=[whole(a) for a in ins],
                out_specs=pl.BlockSpec((OWN_COLS, ROWS), lambda i, _: (0, 0)),
                scratch_shapes=scratch,
            ),
            out_shape=jax.ShapeDtypeStruct((OWN_COLS, ROWS), F32),
            compiler_params=pltpu.CompilerParams(vmem_limit_bytes=VMEM_BYTES),
            cost_estimate=pl.CostEstimate(flops=0, bytes_accessed=1, transcendentals=0),
        )(place, *ins)


def local(grads, momentum):
    grads = grads[0, 0]
    momentum_t = momentum[0].T
    shard = lax.axis_index("shard")
    x, yh = shard // 2, shard % 2
    table = table_parts()
    core = lax.axis_index("rep") % 2
    place = jnp.stack([x, yh, shard, core]).astype(jnp.int32)
    steps = Steps(place, grads)
    pairs = [[2 * k, 2 * k + 1] for k in range(4)]

    tiles_up, tiles_down = (21 - NA, NB), (21, 22 + NA)
    counts_up, counts_down = (NA, MIDDLE - NA), (NA + 1, MIDDLE - NA)

    def around(step, which, pair, after=()):
        name = "ab"[which] + str(step)
        slices = [
            (-1 - step, tiles_up[which], 0, counts_up[which]),
            (1 + step, tiles_down[which], 0, counts_down[which]),
        ]
        out = [counts_up[which], counts_down[which]]
        plus, minus = steps("add_" + name, later_body, slices, pair, out, after)
        return up(name, plus), down(name, minus)

    def cross(rounds):
        name = "cross" + "".join(map(str, rounds))
        slices = []
        for n in rounds:
            slices += [
                (-1 - n, SUPER - NB, NB - SUPER, NBP),
                (1 + n, SUPER - NB + NBP, NB - SUPER, NB - NBP),
            ]
        sent = steps("read_" + name, read_body, slices, [], [len(rounds) * NB])
        return across(name, sent[0])

    def outer(k, came, pair=(), after=()):
        slices = [(-1 - k, 0, SUPER - NB, NBP), (1 + k, NBP, SUPER - NB, NB - NBP)]
        body = functools.partial(outer_body, k % 2 * NB)
        plus, minus = steps(
            f"add_outer{k}", body, slices, [came, *pair], [NBP, NB - NBP], after
        )
        return up(f"outer{k}", plus), down(f"outer{k}", minus)

    slices, out = [], []
    for which in range(2):
        slices += [
            (-1, tiles_up[which], 0, counts_up[which]),
            (1, tiles_down[which], 0, counts_down[which]),
        ]
        out += [counts_up[which], counts_down[which]]
    plus_a, minus_a, plus_b, minus_b = steps("read_first", read_body, slices, [], out)
    a = up("a0", plus_a), down("a0", minus_a)
    b = up("b0", plus_b), down("b0", minus_b)
    y01 = cross((0, 1))
    y23 = cross((2, 3))
    a = around(1, 0, a)
    b = around(1, 1, b)
    a = around(2, 0, a)
    o = outer(0, y01, after=b)
    b = around(2, 1, b, after=a)
    ca = across("a", steps("mix_a", mix_a_body, [(0, 21, -NA, NA + 1)], a, [NA + 1])[0])
    o = outer(1, y01, o, after=[y23])
    mixed = steps(
        "mix_b", mix_b_body, [(0, 22 + NA, NB - 22 - NA, MIDDLE - NA)], b, [MIDDLE - NA]
    )
    cb = across("b", mixed[0])
    o = outer(2, y23, o, after=b)

    near, far = NA * LANES + 64, (MIDDLE - NA) * LANES
    groups = [
        (((21 - NA) * LANES, 0), 0, near),
        ((NB * LANES, near), near // 8, far),
        ((0, (SUPER - NB) * LANES - OWN_COLS), (near + far) // 8, NB * LANES),
    ]
    wide = lambda n, *refs: [[(r, t) for r in refs] for t in range(n)]
    plan = [[(0, NB + t), (1, t) if t < NBP else (2, t - NBP)] for t in range(NB)]
    sides = (wide(NA, 0, 2) + [[(1, 0), (2, NA)]], wide(NA + 1, 1, 2))
    new_t, coeffs = merge_call(
        "merge_a", steps, [], momentum_t, table, groups[0][1],
        [((0, 21 - NA, NA, NA + 1), groups[0][0], near, sides, [*a, ca])],
    )
    sides = (wide(MIDDLE - NA, 0, 2), wide(MIDDLE - NA, 1, 2))
    new_t, coeffs = merge_call(
        "merge_rest", steps, [new_t, coeffs], momentum_t, table, groups[1][1],
        [
            ((0, NB, 22 + NA - NB, MIDDLE - NA), groups[1][0], far, sides, [*b, cb]),
            ((0, 0, SUPER - NB, NB), groups[2][0], NB * LANES, (plan, plan), [y23, *o]),
        ],
    )
    half = PACKED // 2
    part = lambda c: lax.dynamic_slice(coeffs, (c * half, 0), (half, LANES))
    mine = part(core) + send("sum_core", part(1 - core), "rep", CORE_FLIP)
    came = [send(f"sum_z{k}", mine, "rep", z_shift(k)) for k in (2, 1, 3)]
    mine = mine + came[0] + came[1] + came[2]
    mine = mine + send("sum_y", mine, "rep", YLO_FLIP)
    other = send("gather_core", mine, "rep", CORE_FLIP)
    update_t = output_call(
        "update", functools.partial(update_kernel, groups), place, [mine, other, table],
        [pltpu.VMEM((PACKED, LANES), F32)],
    )
    return new_t.T[None], update_t.T


def solution(mesh):
    placed = (P("rep", "shard", None, None), P("rep", None, "shard"))
    return jax.shard_map(
        local,
        mesh=mesh,
        in_specs=placed,
        out_specs=(P("rep", None, "shard"), P(None, "shard")),
        check_vma=False,
    )
```
